768 devices in a mesh: dp: 2 (over core), expert: 12 (over z), tensor: 32 (over y, x).
Axes of the slice: x: 4, y: 8, z: 12, core: 2. Of those that a mesh axis runs over, the one named last changes fastest.
Arguments:
- grad_out: bfloat16 [6144, 4096], P(('dp', 'expert'), 'tensor'), may hold values from -6 to 6
- gates: float32 [6144, 2], P(('dp', 'expert')), may hold values from 0.1 to 1
- routes: int32 [6144, 2], P(('dp', 'expert')), may hold values from 0 to 11, all different within a row; in each aligned block of 256 rows (0 to 255, 256 to 511, ...) at most 64 rows name the same one
- hidden: bfloat16 [2, 12, 768, 4096], P('dp', 'expert'), may hold values from -6 to 6
- w_down: bfloat16 [12, 4096, 4096], P('expert', None, 'tensor'), may hold values from -0.09375 to 0.09375
Outputs:
- hidden_grad: bfloat16 [2, 12, 4096, 768], P('dp', 'expert', 'tensor')
- weight_grad: bfloat16 [12, 4096, 4096], P('expert', 'dp', 'tensor')
The draws below stay inside these ranges and needn't reach their ends.
Inputs may be any that keep to these rules, and one draw needn't show every extreme that they name: `routes`: each token names two different experts; within the tokens of one data group (aligned blocks of 256 tokens) no expert is named more than 64 times, a bound that some block reaches.
All inputs are finite; a program needn't handle non-finite values.
Results may differ from the reference program's by a relative error of at most 0.0059.
Values may be sent and summed in bfloat16 or wider, within the bound.
A program may use at most 64 MiB of HBM per device.

```python
import math
import jax
import jax.numpy as jnp
import numpy as np
from jax import lax

D = 4096
FFE = 4096
TOK_DEV = 256
EXPERTS = 12
CAP = 64
SLOTS = 768
TOKENS = 6144
N_DP = 2
N_EXPERT = 12


def steps_of(stream_key, shape, pieces, low, largest):
    level = 1.0
    for dim, shards_of in pieces:
        steps = jax.random.uniform(jax.random.fold_in(jax.random.fold_in(stream_key, 6), dim), (shards_of,), jnp.float32, low / len(pieces), largest / len(pieces))
        level = level * jnp.repeat(jnp.exp(steps), shape[dim] // shards_of).reshape((-1,) + (1,) * (len(shape) - 1 - dim))
    return level


def deal_out(own_key, own, number, rows, amount, top, most, skew):
    order = jax.random.permutation(own_key, amount)
    heavy_load, usual = load_shares(amount, rows * top, most, skew, True), load_shares(amount, rows * top, most, skew, False)
    places = jnp.arange(amount)

    def named(tallies, offset_by):
        used = int((tallies > 0).sum())
        fixed = max(1, used // 4)
        moved = fixed + (places - fixed + offset_by * (used - fixed)) % max(1, amount - fixed)
        return jnp.zeros((amount,), jnp.int32).at[order[jnp.where(places < fixed, places, moved)]].set(jnp.asarray(tallies, jnp.int32))

    tallies = jnp.where(number % 4 == 0, named(heavy_load, number // 4), named(usual, number - number // 4 - 1))
    mixed = jax.random.permutation(jax.random.fold_in(own, 3), amount)
    donor, taker = mixed[0:amount // 2 * 2:2], mixed[1:amount // 2 * 2:2]
    room = jnp.minimum(tallies[donor] - 1, most - tallies[taker]) // 2
    room = jnp.where((donor == order[0]) | (taker == order[0]) | (tallies[taker] == 0), 0, jnp.maximum(room, 0))
    moved = jax.random.randint(jax.random.fold_in(own, 4), (amount // 2,), 0, 1 << 20) % (room + 1)
    tallies = tallies.at[donor].add(-moved).at[taker].add(moved)
    members = jnp.searchsorted(jnp.cumsum(tallies), jnp.arange(rows * top), side="right").astype(jnp.int32)
    grid = members.reshape(top, rows).T
    grid = grid[jax.random.permutation(jax.random.fold_in(own, 1), rows)]
    offset_by = jax.random.randint(jax.random.fold_in(own, 2), (rows, 1), 0, top)
    return jnp.take_along_axis(grid, (jnp.arange(top)[None, :] + offset_by) % top, axis=1)


def load_shares(amount, total, reach, lean, full):
    loads = [(1 << 20) // math.isqrt(rank ** lean) + 1 for rank in range(1, amount + 1)]
    largest = reach if full else min(reach, max(-(-total // amount), total * loads[0] // sum(loads)))
    least = 1 if total - largest >= amount - 1 else 0
    counts, rest = [largest] + [least] * (amount - 1), total - largest - least * (amount - 1)
    while rest > 0:
        free = [i for i in range(1, amount) if counts[i] < largest] or [i for i in range(1, amount) if counts[i] < reach]
        pool, remaining = sum([loads[i] for i in free]), rest
        for i in free:
            addition = min(reach - counts[i], max(1, remaining * loads[i] // pool), rest)
            counts[i] = counts[i] + addition
            rest = rest - addition
    return np.array(counts)


def bell_draw(own_key, dims, spread, limit, cuts=(), kind=jnp.bfloat16):
    entries = jax.random.normal(own_key, dims, jnp.float32) * spread
    if len(cuts) > 0:
        entries = steps_of(own_key, dims, cuts, -0.22, 0.18) * entries
    return jnp.clip(entries, min=-limit, max=limit).astype(kind)


def setup_inputs(seed: int = 0) -> dict:
    key_of = jax.random.split(jax.random.key(seed), 6)
    grad_out = bell_draw(key_of[0], (TOKENS, D), 1.0, 6.0, ((0, 24), (1, 32)))
    gates = jnp.clip(0.1 + 0.9 * jax.random.uniform(key_of[1], (TOKENS, 2), jnp.float32) ** steps_of(key_of[1], (TOKENS, 2), ((0, 24),), -0.2, 0.2), 0.1, 1.0)
    routes_keys = jax.random.split(jax.random.fold_in(key_of[2], 1), TOKENS // TOK_DEV)
    routes_turns = jax.random.permutation(jax.random.fold_in(key_of[2], 3), TOKENS // TOK_DEV)
    routes = jax.vmap(lambda own, number: deal_out(jax.random.fold_in(key_of[2], 2), own, number, TOK_DEV, EXPERTS, 2, CAP, 1))(routes_keys, routes_turns).reshape((TOKENS, 2))
    hidden = bell_draw(key_of[3], (N_DP, EXPERTS, SLOTS, FFE), 1.0, 6.0, ((0, 2), (1, 12)))
    w_down = bell_draw(key_of[4], (EXPERTS, FFE, D), FFE ** -0.5, 0.09375, ((0, 12), (2, 32)))
    return {"grad_out": grad_out, "gates": gates, "routes": routes, "hidden": hidden, "w_down": w_down}


def reference(grad_out, gates, routes, hidden, w_down):
    group_count = N_DP * N_EXPERT
    group_rows = 2 * TOK_DEV
    slot_count = N_EXPERT * CAP
    chosen = routes.reshape(group_count, group_rows)
    onehot = (chosen[:, :, None] == jnp.arange(N_EXPERT, dtype=jnp.int32)[None, None, :]).astype(jnp.int32)
    before = jnp.cumsum(onehot, axis=1) - onehot
    position = jnp.sum(before * onehot, axis=2)
    slot = chosen * CAP + position
    offsets = (jnp.arange(group_count, dtype=jnp.int32) * group_rows)[:, None]
    empty_row = group_count * group_rows

    def fill_group(group_slot, group_base):
        start = jnp.full((slot_count,), empty_row, jnp.int32)
        return start.at[group_slot].set(group_base + jnp.arange(group_rows, dtype=jnp.int32))

    source = jax.vmap(fill_group)(slot, offsets)
    source = source.reshape(N_DP, N_EXPERT, N_EXPERT, CAP)
    scaled = (gates[:, :, None] * grad_out[:, None, :].astype(jnp.float32)).reshape(group_count * group_rows, D)
    scaled = scaled.astype(jnp.bfloat16)
    padded = jnp.concatenate([scaled, jnp.zeros((1, D), jnp.bfloat16)], axis=0)

    def per_expert(expert_id):
        picked = jnp.take(source, expert_id, axis=2).reshape(N_DP, slot_count)
        arrived = jnp.take(padded, picked, axis=0).astype(jnp.float32)
        weight = jnp.take(w_down, expert_id, axis=0).astype(jnp.float32)
        saved = jnp.take(hidden, expert_id, axis=1).astype(jnp.float32)
        grad_hidden = jnp.einsum('fd,psd->pfs', weight, arrived).astype(jnp.bfloat16)
        partial_sums = jnp.einsum('psf,psd->pfd', saved, arrived).astype(jnp.bfloat16)
        partial_sums = lax.optimization_barrier(partial_sums).astype(jnp.float32)
        grad_weight = jnp.sum(partial_sums, axis=0).astype(jnp.bfloat16)
        return grad_hidden, grad_weight

    grad_hidden, grad_weight = lax.map(per_expert, jnp.arange(EXPERTS, dtype=jnp.int32))
    return jnp.transpose(grad_hidden, (1, 0, 2, 3)), grad_weight
```

```python
import functools

import jax
import jax.numpy as jnp
from jax import lax
from jax.experimental import pallas as pl
from jax.experimental.pallas import tpu as pltpu
from jax.sharding import PartitionSpec as P

MESH = pl.DeviceIdType.MESH
RING_X = 4
CHUNKS = 4
PIECES = 8


def kernel(
    ring_e,
    ring_x,
    ring_y,
    grad_ref,
    gates_ref,
    routes_ref,
    hidden_ref,
    w_ref,
    hg_ref,
    wg_ref,
    saved,
    weight,
    arrived,
    outgoing,
    place,
    gate_of,
    flipped,
    prod,
    part_out,
    part_in,
    local,
    other,
    saved_sem,
    own_sem,
    z_send,
    z_recv,
    w_send,
    w_recv,
    f_send,
    f_recv,
    x_send,
    x_recv,
    r_send,
    r_recv,
    y_send,
    y_recv,
    g_send,
    g_recv,
):
    tokens = grad_ref.shape[0]
    cap = arrived.shape[2]
    features = arrived.shape[3]
    group = ring_e // CHUNKS
    rows = group * cap
    half_y = ring_y // 2
    units = prod.shape[3]
    half_units = other.shape[0]

    core = lax.axis_index("dp")
    me = lax.axis_index("expert")
    flat = lax.axis_index("tensor")
    y, x = flat // ring_x, lax.rem(flat, ring_x)
    sibling = {"dp": 1 - core}

    def at_x(step):
        return {"tensor": y * ring_x + lax.rem(x + step + ring_x, ring_x)}

    def at_y(step):
        return {"tensor": lax.rem(y + step + ring_y, ring_y) * ring_x + x}

    def peer(number):
        offset = (number + 1) // 2 if number % 2 else -(number // 2)
        return lax.rem(me + offset + ring_e, ring_e)

    def mirror(number):
        if number == ring_e - 1:
            return number
        return number + 1 if number % 2 else number - 1

    def send(src, dst, send_sem, recv_sem, where):
        return pltpu.make_async_remote_copy(
            src_ref=src,
            dst_ref=dst,
            send_sem=send_sem,
            recv_sem=recv_sem,
            device_id=where,
            device_id_type=MESH,
        )

    barrier = pltpu.get_barrier_semaphore()
    for number in range(1, ring_e):
        pl.semaphore_signal(
            barrier, inc=1, device_id={"expert": peer(number)}, device_id_type=MESH
        )
    for step in (1, -1, 2):
        pl.semaphore_signal(barrier, inc=1, device_id=at_x(step), device_id_type=MESH)
    for step in (1, -1):
        pl.semaphore_signal(barrier, inc=1, device_id=at_y(step), device_id_type=MESH)
    pl.semaphore_signal(barrier, inc=1, device_id=sibling, device_id_type=MESH)

    own = pltpu.make_async_copy(w_ref.at[:, x], weight.at[0], own_sem)
    own.start()
    saved_copies = []
    for number in range(ring_e):
        copy = pltpu.make_async_copy(
            hidden_ref.at[peer(number)],
            saved.at[pl.ds(number * cap, cap)],
            saved_sem.at[number],
        )
        copy.start()
        saved_copies.append(copy)

    sublanes = place.shape[0]
    expert_ids = lax.broadcasted_iota(jnp.int32, (sublanes, tokens), 0)
    first = routes_ref[0:1, :] == expert_ids
    second = routes_ref[1:2, :] == expert_ids
    member = jnp.where(first | second, 1.0, 0.0).astype(jnp.bfloat16)
    earlier = jnp.where(
        lax.broadcasted_iota(jnp.int32, (tokens, tokens), 0)
        < lax.broadcasted_iota(jnp.int32, (tokens, tokens), 1),
        1.0,
        0.0,
    ).astype(jnp.bfloat16)
    before = jnp.dot(member, earlier, preferred_element_type=jnp.float32)
    place[...] = jnp.where(first | second, before.astype(jnp.int32), -1)
    gate_of[...] = jnp.where(first, gates_ref[0:1, :], 0.0) + jnp.where(
        second, gates_ref[1:2, :], 0.0
    )

    pl.semaphore_wait(barrier, ring_e - 1 + 3 + 2 + 1)

    half_rows = pl.ds(core * half_y, half_y)
    w_copies = {}
    for step, slot in ((1, 1), (-1, 3), (2, 2)):
        copy = send(
            w_ref.at[half_rows, lax.rem(x + step + ring_x, ring_x)],
            weight.at[slot, half_rows],
            w_send.at[slot],
            w_recv.at[slot],
            at_x(step),
        )
        copy.start()
        w_copies[slot] = copy

    z_copies = {}
    slot_ids = lax.broadcasted_iota(jnp.int32, (cap, tokens), 0)
    for chunk in range(CHUNKS):
        masks, scales = [], []
        numbers = range(chunk * group, (chunk + 1) * group)
        for number in numbers:
            expert = peer(number)
            hit = slot_ids == place[pl.ds(expert, 1), :]
            masks.append(jnp.where(hit, 1.0, 0.0).astype(jnp.bfloat16))
            scales.append(
                jnp.sum(
                    jnp.where(hit, gate_of[pl.ds(expert, 1), :], 0.0), axis=1, keepdims=True
                )
            )
        picked = jnp.dot(
            jnp.concatenate(masks, axis=0), grad_ref[...], preferred_element_type=jnp.float32
        )
        scaled = (jnp.concatenate(scales, axis=0) * picked).astype(jnp.bfloat16)
        for index, number in enumerate(numbers):
            block = scaled[index * cap : (index + 1) * cap]
            if number == 0:
                arrived[0, 0] = block
                continue
            outgoing[number] = block
            copy = send(
                outgoing.at[number],
                arrived.at[0, mirror(number)],
                z_send.at[number],
                z_recv.at[mirror(number)],
                {"expert": peer(number)},
            )
            copy.start()
            z_copies[number] = copy

    x_copies, r_copies, f_copies, y_copies = {}, {}, {}, {}

    def gather(chunk):
        blocks = pl.ds(chunk * group, group)
        for number in range(chunk * group, (chunk + 1) * group):
            if number > 0:
                z_copies[mirror(number)].wait_recv()
        for step, slot, lane in ((1, 1, 0), (-1, 3, 1)):
            copy = send(
                arrived.at[0, blocks],
                arrived.at[slot, blocks],
                x_send.at[chunk, lane],
                x_recv.at[chunk, lane],
                at_x(step),
            )
            copy.start()
            x_copies[chunk, lane] = copy

    def relay(chunk):
        blocks = pl.ds(chunk * group, group)
        lane = chunk % 2
        x_copies[chunk, lane].wait_recv()
        copy = send(
            arrived.at[(1, 3)[lane], blocks],
            arrived.at[2, blocks],
            r_send.at[chunk],
            r_recv.at[chunk],
            at_x((1, -1)[lane]),
        )
        copy.start()
        r_copies[chunk] = copy

    def share_weight():
        own.wait()
        for slot in (1, 3, 2):
            w_copies[slot].wait_recv()
            copy = send(
                weight.at[slot, half_rows],
                weight.at[slot, half_rows],
                f_send.at[slot],
                f_recv.at[slot],
                sibling,
            )
            copy.start()
            f_copies[slot] = copy
        for slot in (1, 3, 2):
            f_copies[slot].wait_recv()

    def product(chunk):
        x_copies[chunk, 1 - chunk % 2].wait_recv()
        r_copies[chunk].wait_recv()
        blocks = pl.ds(chunk * group, group)
        left = jnp.concatenate(
            [arrived[slot, blocks].reshape(rows, features) for slot in range(ring_x)], axis=1
        )
        for pair in range(half_y):
            right = []
            for number in (2 * pair, 2 * pair + 1):
                target = lax.rem(y + number - (half_y - 1) + ring_y, ring_y)
                right.append(
                    jnp.concatenate([weight[slot, target] for slot in range(ring_x)], axis=1)
                )
            both = lax.dot_general(
                left,
                jnp.concatenate(right, axis=0),
                (((1,), (1,)), ((), ())),
                preferred_element_type=jnp.float32,
            )
            prod[chunk, 2 * pair] = both[:, :units]
            prod[chunk, 2 * pair + 1] = both[:, units:]

    def first_step(chunk, lane):
        return 0 if chunk % 2 == lane else 1

    def reduce_step(chunk, lane, step):
        distance = half_y - step if lane == 0 else step - half_y
        number = distance + half_y - 1
        if number < 0:
            number += ring_y
        total = prod[chunk, number]
        if step > first_step(chunk, lane):
            y_copies[lane, chunk, step - 1].wait_recv()
            total = total + part_in[lane, chunk, step - 1].astype(jnp.float32)
        part_out[lane, chunk, step] = total.astype(jnp.bfloat16)
        copy = send(
            part_out.at[lane, chunk, step],
            part_in.at[lane, chunk, step],
            y_send.at[lane, chunk, step],
            y_recv.at[lane, chunk, step],
            at_y((1, -1)[lane]),
        )
        copy.start()
        y_copies[lane, chunk, step] = copy

    def start_reduce(chunk):
        for lane in (chunk % 2, 1 - chunk % 2):
            reduce_step(chunk, lane, first_step(chunk, lane))

    def finish(chunk):
        last = half_y - 1
        y_copies[0, chunk, last].wait_recv()
        y_copies[1, chunk, last].wait_recv()
        total = (
            prod[chunk, half_y - 1]
            + part_in[0, chunk, last].astype(jnp.float32)
            + part_in[1, chunk, last].astype(jnp.float32)
        ).astype(jnp.bfloat16)
        for index in range(group):
            source = peer(chunk * group + index)
            hg_ref[pl.ds(pl.multiple_of(source * cap, cap), cap), :] = total[
                index * cap : (index + 1) * cap
            ]

    piece_units = local.shape[0] // PIECES

    def weight_piece(piece):
        if piece == 0:
            for copy in saved_copies:
                copy.wait()
            flipped[...] = arrived[0].reshape(ring_e * cap, features).T
        base = (1 - core) * half_units if piece < PIECES // 2 else core * half_units
        start = base + (piece % (PIECES // 2)) * piece_units
        start = pl.multiple_of(start, piece_units)
        block = jnp.dot(
            flipped[...],
            saved[:, pl.ds(start, piece_units)],
            preferred_element_type=jnp.float32,
        )
        local[pl.ds(start, piece_units), :] = block.T.astype(jnp.bfloat16)

    theirs = pl.ds(pl.multiple_of((1 - core) * half_units, half_units), half_units)
    ours = pl.ds(pl.multiple_of(core * half_units, half_units), half_units)
    swap = send(local.at[theirs], other, g_send, g_recv, sibling)

    def advance(pieces):
        piece = next(pieces, None)
        if piece is not None:
            weight_piece(piece)
            if piece == PIECES // 2 - 1:
                swap.start()

    gather(0)
    gather(1)
    relay(0)
    gather(2)
    relay(1)
    share_weight()
    product(0)
    start_reduce(0)
    gather(3)
    relay(2)
    product(1)
    start_reduce(1)
    relay(3)
    product(2)
    start_reduce(2)
    product(3)
    start_reduce(3)

    pieces = iter(range(PIECES))
    for step in range(1, half_y):
        for chunk in range(CHUNKS):
            for lane in (0, 1):
                if step > first_step(chunk, lane):
                    reduce_step(chunk, lane, step)
            advance(pieces)
    for _ in range(PIECES):
        advance(pieces)
    for chunk in range(CHUNKS):
        finish(chunk)

    swap.wait_recv()
    wg_ref[...] = (local[ours].astype(jnp.float32) + other[...].astype(jnp.float32)).astype(
        jnp.bfloat16
    )

    for copies in (w_copies, z_copies, x_copies, r_copies, f_copies, y_copies):
        for copy in copies.values():
            copy.wait_send()
    swap.wait_send()


def per_device(grad_out, gates, routes, hidden, w_down):
    ring_e = lax.axis_size("expert")
    ring_t = lax.axis_size("tensor")
    ring_x = RING_X
    ring_y = ring_t // ring_x
    tokens, features = grad_out.shape
    slots, units = hidden.shape[2], hidden.shape[3]
    cap = slots // ring_e
    own_units = units // ring_t
    rows = slots // CHUNKS
    half_y = ring_y // 2
    sublanes = -(-ring_e // 16) * 16
    bf16, f32 = jnp.bfloat16, jnp.float32
    dma = pltpu.SemaphoreType.DMA
    vmem = pl.BlockSpec(memory_space=pltpu.VMEM)
    hbm = pl.BlockSpec(memory_space=pl.ANY)
    hidden_grad, weight_grad = pl.pallas_call(
        functools.partial(kernel, ring_e, ring_x, ring_y),
        out_shape=(
            jax.ShapeDtypeStruct((slots, own_units), bf16),
            jax.ShapeDtypeStruct((units // 2, features), bf16),
        ),
        in_specs=[vmem, vmem, vmem, hbm, hbm],
        out_specs=(vmem, vmem),
        scratch_shapes=[
            pltpu.VMEM((slots, units), bf16),
            pltpu.VMEM((ring_x, ring_y, own_units, features), bf16),
            pltpu.VMEM((ring_x, ring_e, cap, features), bf16),
            pltpu.VMEM((ring_e, cap, features), bf16),
            pltpu.VMEM((sublanes, tokens), jnp.int32),
            pltpu.VMEM((sublanes, tokens), f32),
            pltpu.VMEM((features, slots), bf16),
            pltpu.VMEM((CHUNKS, ring_y, rows, own_units), f32),
            pltpu.VMEM((2, CHUNKS, half_y, rows, own_units), bf16),
            pltpu.VMEM((2, CHUNKS, half_y, rows, own_units), bf16),
            pltpu.VMEM((units, features), bf16),
            pltpu.VMEM((units // 2, features), bf16),
            dma((ring_e,)),
            dma,
            dma((ring_e,)),
            dma((ring_e,)),
            dma((ring_x,)),
            dma((ring_x,)),
            dma((ring_x,)),
            dma((ring_x,)),
            dma((CHUNKS, 2)),
            dma((CHUNKS, 2)),
            dma((CHUNKS,)),
            dma((CHUNKS,)),
            dma((2, CHUNKS, half_y)),
            dma((2, CHUNKS, half_y)),
            dma,
            dma,
        ],
        compiler_params=pltpu.CompilerParams(
            collective_id=0, has_side_effects=True, vmem_limit_bytes=40 * 1024 * 1024
        ),
        cost_estimate=pl.CostEstimate(
            flops=4 * units * slots * features,
            bytes_accessed=2 * units * (slots + 2 * features),
            transcendentals=0,
        ),
    )(
        grad_out,
        gates.T,
        routes.T,
        hidden.reshape(ring_e, cap, units),
        w_down.reshape(ring_y, ring_x, own_units, features),
    )
    return hidden_grad.T[None, None], weight_grad[None]


def solution(mesh):
    placed = (
        P(("dp", "expert"), "tensor"),
        P(("dp", "expert"), None),
        P(("dp", "expert"), None),
        P("dp", "expert", None, None),
        P("expert", None, "tensor"),
    )
    return jax.shard_map(
        per_device,
        mesh=mesh,
        in_specs=placed,
        out_specs=(P("dp", "expert", "tensor", None), P("expert", "dp", "tensor")),
        check_vma=False,
    )
```

```python
import functools

import jax
import jax.numpy as jnp
from jax import lax
from jax.experimental import pallas as pl
from jax.experimental.pallas import tpu as pltpu
from jax.sharding import PartitionSpec as P

MESH = pl.DeviceIdType.MESH
RING_X = 4
CHUNKS = 4
PIECES = 8
BOUNDS = [0, 3, 5, 8]
SCHEDULE = tuple(
    step
    for steps in (
        ("W0", "W1", "W2", "g0", "g1", "g2", "g3", "s0", "s1"),
        ("s2", "a", "a", "p00", "S0", "p10", "S1", "p20", "S2"),
        ("p30", "S3", "a", "L0", "a", "L1", "a", "L2", "a"),
        ("L3", "p01", "B02", "a", "p11", "B12", "a", "p21", "B22"),
        ("p31", "B32", "p02", "B03", "p12", "B13", "p22", "B23", "p32"),
        ("B33",),
    )
    for step in steps
)


def kernel(
    ring_e,
    ring_x,
    ring_y,
    grad_hbm,
    gates_hbm,
    routes_hbm,
    hidden_ref,
    w_ref,
    hg_hbm,
    wg_hbm,
    grad_ref,
    gates_ref,
    routes_ref,
    saved,
    staged,
    weight,
    arrived,
    outgoing,
    place,
    gate_of,
    flipped,
    prod,
    part_out,
    part_in,
    local,
    other,
    gathered_grad,
    hg_ref,
    wg_ref,
    small_sem,
    saved_sem,
    staged_sem,
    z_send,
    z_recv,
    w_send,
    w_recv,
    f_send,
    f_recv,
    x_send,
    x_recv,
    y_send,
    y_recv,
    g_send,
    g_recv,
    out_sem,
):
    tokens = grad_ref.shape[0]
    cap = arrived.shape[2]
    features = arrived.shape[3]
    group = ring_e // CHUNKS
    rows = group * cap
    half_y = ring_y // 2
    units = prod.shape[3]
    half_units = other.shape[0]

    core = lax.axis_index("dp")
    me = lax.axis_index("expert")
    flat = lax.axis_index("tensor")
    y, x = flat // ring_x, lax.rem(flat, ring_x)
    sibling = {"dp": 1 - core}

    def at_x(step):
        return {"tensor": y * ring_x + lax.rem(x + step + ring_x, ring_x)}

    def at_y(step):
        return {"tensor": lax.rem(y + step + ring_y, ring_y) * ring_x + x}

    offsets = [0, 1, -1, ring_e // 2]
    for offset in range(ring_e // 2 - 1, 1, -1):
        offsets += [offset, -offset]

    def peer(number):
        return lax.rem(me + offsets[number] + ring_e, ring_e)

    def mirror(number):
        if 2 * offsets[number] == ring_e:
            return number
        return offsets.index(-offsets[number])

    def send(src, dst, send_sem, recv_sem, where):
        return pltpu.make_async_remote_copy(
            src_ref=src,
            dst_ref=dst,
            send_sem=send_sem,
            recv_sem=recv_sem,
            device_id=where,
            device_id_type=MESH,
        )

    barrier = pltpu.get_barrier_semaphore()
    for number in range(1, ring_e):
        pl.semaphore_signal(
            barrier, inc=1, device_id={"expert": peer(number)}, device_id_type=MESH
        )
    for step in (1, -1, 2):
        pl.semaphore_signal(barrier, inc=1, device_id=at_x(step), device_id_type=MESH)
    for step in (1, -1):
        pl.semaphore_signal(barrier, inc=1, device_id=at_y(step), device_id_type=MESH)
    pl.semaphore_signal(barrier, inc=1, device_id=sibling, device_id_type=MESH)

    small = [
        pltpu.make_async_copy(src, dst, small_sem.at[index])
        for index, (src, dst) in enumerate(
            ((routes_hbm, routes_ref), (gates_hbm, gates_ref), (grad_hbm, grad_ref))
        )
    ]
    for copy in small:
        copy.start()

    distances = [4, 3, -3, 2, -2, 1, -1, 0]
    bounds = BOUNDS
    parts = [pl.ds(a, b - a) for a, b in zip(bounds, bounds[1:])]
    staged_copies = []
    for index, distance in enumerate(distances):
        copy = pltpu.make_async_copy(
            w_ref.at[lax.rem(y + distance + ring_y, ring_y)],
            staged.at[index],
            staged_sem.at[index],
        )
        copy.start()
        staged_copies.append(copy)
    small[0].wait()
    small[1].wait()

    sublanes = place.shape[0]
    expert_ids = lax.broadcasted_iota(jnp.int32, (sublanes, tokens), 0)
    first = routes_ref[0:1, :] == expert_ids
    second = routes_ref[1:2, :] == expert_ids
    member = jnp.where(first | second, 1.0, 0.0).astype(jnp.bfloat16)
    earlier = jnp.where(
        lax.broadcasted_iota(jnp.int32, (tokens, tokens), 0)
        < lax.broadcasted_iota(jnp.int32, (tokens, tokens), 1),
        1.0,
        0.0,
    ).astype(jnp.bfloat16)
    before = jnp.dot(member, earlier, preferred_element_type=jnp.float32)
    place[...] = jnp.where(first | second, before.astype(jnp.int32), -1)
    gate_of[...] = jnp.where(first, gates_ref[0:1, :], 0.0) + jnp.where(
        second, gates_ref[1:2, :], 0.0
    )

    small[2].wait()

    slot_ids = lax.broadcasted_iota(jnp.int32, (cap, tokens), 0)
    for chunk in range(CHUNKS):
        masks, scales = [], []
        numbers = range(chunk * group, (chunk + 1) * group)
        for number in numbers:
            expert = peer(number)
            hit = slot_ids == place[pl.ds(expert, 1), :]
            masks.append(jnp.where(hit, 1.0, 0.0).astype(jnp.bfloat16))
            scales.append(
                jnp.sum(
                    jnp.where(hit, gate_of[pl.ds(expert, 1), :], 0.0), axis=1, keepdims=True
                )
            )
        picked = jnp.dot(
            jnp.concatenate(masks, axis=0), grad_ref[...], preferred_element_type=jnp.float32
        )
        scaled = (jnp.concatenate(scales, axis=0) * picked).astype(jnp.bfloat16)
        for index, number in enumerate(numbers):
            block = scaled[index * cap : (index + 1) * cap]
            if number == 0:
                arrived[0, 0] = block
            else:
                outgoing[number] = block

    pl.semaphore_wait(barrier, ring_e - 1 + 3 + 2 + 1)

    z_copies = {}
    for number in range(1, ring_e):
        copy = send(
            outgoing.at[number],
            arrived.at[0, mirror(number)],
            z_send.at[number],
            z_recv.at[mirror(number)],
            {"expert": peer(number)},
        )
        copy.start()
        z_copies[number] = copy

    half_rows = pl.ds(pl.multiple_of(core * (units // 2), units // 2), units // 2)
    w_copies = {}
    for copy in staged_copies:
        copy.wait()

    def chip(step):
        return lax.rem(x + step + ring_x, ring_x)

    def send_weight(number):
        part = parts[number]
        for lane, step, slot in ((4, 2, 1), (0, 1, 0), (1, -1, 2)):
            copy = send(
                staged.at[part, chip(step), half_rows],
                weight.at[slot, part, half_rows],
                w_send.at[number, lane],
                w_recv.at[number, lane],
                at_x(step),
            )
            copy.start()
            w_copies[number, lane] = copy

    saved_copies = []
    for number in range(ring_e):
        copy = pltpu.make_async_copy(
            hidden_ref.at[peer(number)],
            saved.at[pl.ds(number * cap, cap)],
            saved_sem.at[number],
        )
        copy.start()
        saved_copies.append(copy)

    x_copies, f_copies, y_copies = {}, {}, {}

    def gather(chunk):
        blocks = pl.ds(chunk * group, group)
        for number in range(chunk * group, (chunk + 1) * group):
            if number > 0:
                z_copies[mirror(number)].wait_recv()
        for step, slot in ((2, 2), (1, 1), (-1, 3)):
            copy = send(
                arrived.at[0, blocks],
                arrived.at[slot, blocks],
                x_send.at[chunk, slot],
                x_recv.at[chunk, slot],
                at_x(step),
            )
            copy.start()
            x_copies[chunk, slot] = copy

    def share_weight(number):
        part = parts[number]
        for slot, needed in ((0, (0,)), (2, (1,)), (1, (4,))):
            for lane in needed:
                w_copies[number, lane].wait_recv()
            copy = send(
                weight.at[slot, part, half_rows],
                weight.at[slot, part, half_rows],
                f_send.at[number, slot],
                f_recv.at[number, slot],
                sibling,
            )
            copy.start()
            f_copies[number, slot] = copy

    gathered, shared = set(), set()

    def product(chunk, number):
        if chunk not in gathered:
            gathered.add(chunk)
            for slot in range(1, ring_x):
                x_copies[chunk, slot].wait_recv()
        if number not in shared:
            shared.add(number)
            for slot in range(ring_x - 1):
                f_copies[number, slot].wait_recv()
        blocks = pl.ds(chunk * group, group)
        left = jnp.concatenate(
            [arrived[slot, blocks].reshape(rows, features) for slot in range(ring_x)], axis=1
        )
        right = []
        first, end = bounds[number], bounds[number + 1]
        for index in range(first, end):
            right.append(
                jnp.concatenate(
                    [staged[index, x]] + [weight[slot, index] for slot in range(ring_x - 1)],
                    axis=1,
                )
            )
        product = lax.dot_general(
            left,
            jnp.concatenate(right, axis=0),
            (((1,), (1,)), ((), ())),
            preferred_element_type=jnp.float32,
        )
        for index in range(first, end):
            offset = (index - first) * units
            prod[chunk, index] = product[:, offset : offset + units]

    def message(chunk, lane, slot):
        sign = (1, -1)[lane]
        long = chunk // 2 == lane
        distance = 4 - slot
        takes = (slot - 1,) if slot > (0 if long else 1) else ()
        total = prod[chunk, distances.index(4 if distance == 4 else sign * distance)]
        for taken in takes:
            y_copies[lane, chunk, taken].wait_recv()
            total = total + part_in[lane, chunk, taken].astype(jnp.float32)
        part_out[lane, chunk, slot] = total.astype(jnp.bfloat16)
        copy = send(
            part_out.at[lane, chunk, slot],
            part_in.at[lane, chunk, slot],
            y_send.at[lane, chunk, slot],
            y_recv.at[lane, chunk, slot],
            at_y(sign),
        )
        copy.start()
        y_copies[lane, chunk, slot] = copy

    def start_reduce(chunk):
        long = chunk // 2
        message(chunk, long, 0)
        message(chunk, 1 - long, 1)

    def long_step(chunk):
        message(chunk, chunk // 2, 1)

    def both_step(chunk, slot):
        message(chunk, 0, slot)
        message(chunk, 1, slot)

    def finish(chunk):
        last = 3
        y_copies[0, chunk, last].wait_recv()
        y_copies[1, chunk, last].wait_recv()
        total = (
            prod[chunk, ring_y - 1]
            + part_in[0, chunk, last].astype(jnp.float32)
            + part_in[1, chunk, last].astype(jnp.float32)
        ).astype(jnp.bfloat16)
        for index in range(group):
            source = peer(chunk * group + index)
            gathered_grad[pl.ds(pl.multiple_of(source * cap, cap), cap), :] = total[
                index * cap : (index + 1) * cap
            ]

    piece_units = local.shape[0] // PIECES

    def weight_piece(piece):
        if piece == 0:
            for copy in saved_copies:
                copy.wait()
            flipped[...] = arrived[0].reshape(ring_e * cap, features).T
        base = (1 - core) * half_units if piece < PIECES // 2 else core * half_units
        start = base + (piece % (PIECES // 2)) * piece_units
        start = pl.multiple_of(start, piece_units)
        block = jnp.dot(
            flipped[...],
            saved[:, pl.ds(start, piece_units)],
            preferred_element_type=jnp.float32,
        )
        local[pl.ds(start, piece_units), :] = block.T.astype(jnp.bfloat16)

    theirs = pl.ds(pl.multiple_of((1 - core) * half_units, half_units), half_units)
    ours = pl.ds(pl.multiple_of(core * half_units, half_units), half_units)
    swap = send(local.at[theirs], other, g_send, g_recv, sibling)

    def advance(pieces):
        piece = next(pieces, None)
        if piece is not None:
            weight_piece(piece)
            if piece == PIECES // 2 - 1:
                swap.start()

    pieces = iter(range(PIECES))
    ops = {
        "g": gather,
        "W": send_weight,
        "s": share_weight,
        "p": product,
        "S": start_reduce,
        "L": long_step,
        "B": both_step,
        "f": finish,
        "a": lambda: advance(pieces),
    }
    for op in SCHEDULE:
        ops[op[0]](*[int(digit) for digit in op[1:]])

    swap.wait_recv()
    wg_ref[...] = (local[ours].astype(jnp.float32) + other[...].astype(jnp.float32)).astype(
        jnp.bfloat16
    )
    out = pltpu.make_async_copy(wg_ref, wg_hbm, out_sem.at[1])
    out.start()
    for chunk in range(CHUNKS):
        finish(chunk)
    hg_ref[...] = gathered_grad[...].T
    last_out = pltpu.make_async_copy(hg_ref, hg_hbm, out_sem.at[0])
    last_out.start()
    out.wait()
    last_out.wait()

    for copies in (w_copies, z_copies, x_copies, f_copies, y_copies):
        for copy in copies.values():
            copy.wait_send()
    swap.wait_send()


def hand_over(first_in, second_in, first_out, second_out, first, second, sem):
    pairs = ((first_in, first, first_out), (second_in, second, second_out))
    reads = [
        pltpu.make_async_copy(src, here, sem.at[0, index])
        for index, (src, here, _) in enumerate(pairs)
    ]
    writes = [
        pltpu.make_async_copy(here, dst, sem.at[1, index])
        for index, (_, here, dst) in enumerate(pairs)
    ]
    for read in reads:
        read.start()
    for read, write in zip(reads, writes):
        read.wait()
        write.start()
    for write in writes:
        write.wait()


def per_device(grad_out, gates, routes, hidden, w_down):
    ring_e = lax.axis_size("expert")
    ring_t = lax.axis_size("tensor")
    ring_x = RING_X
    ring_y = ring_t // ring_x
    tokens, features = grad_out.shape
    slots, units = hidden.shape[2], hidden.shape[3]
    cap = slots // ring_e
    own_units = units // ring_t
    rows = slots // CHUNKS
    half_y = ring_y // 2
    sublanes = -(-ring_e // 16) * 16
    bf16, f32 = jnp.bfloat16, jnp.float32
    dma = pltpu.SemaphoreType.DMA
    hbm = pl.BlockSpec(memory_space=pl.ANY)
    hidden_grad, weight_grad = pl.pallas_call(
        functools.partial(kernel, ring_e, ring_x, ring_y),
        out_shape=(
            jax.ShapeDtypeStruct((own_units, slots), bf16),
            jax.ShapeDtypeStruct((units // 2, features), bf16),
        ),
        in_specs=[hbm] * 5,
        out_specs=(hbm, hbm),
        scratch_shapes=[
            pltpu.VMEM((tokens, features), bf16),
            pltpu.VMEM((2, tokens), f32),
            pltpu.VMEM((2, tokens), jnp.int32),
            pltpu.VMEM((slots, units), bf16),
            pltpu.VMEM((ring_y, ring_x, own_units, features), bf16),
            pltpu.VMEM((ring_x - 1, ring_y, own_units, features), bf16),
            pltpu.VMEM((ring_x, ring_e, cap, features), bf16),
            pltpu.VMEM((ring_e, cap, features), bf16),
            pltpu.VMEM((sublanes, tokens), jnp.int32),
            pltpu.VMEM((sublanes, tokens), f32),
            pltpu.VMEM((features, slots), bf16),
            pltpu.VMEM((CHUNKS, ring_y, rows, own_units), f32),
            pltpu.VMEM((2, CHUNKS, half_y, rows, own_units), bf16),
            pltpu.VMEM((2, CHUNKS, half_y, rows, own_units), bf16),
            pltpu.VMEM((units, features), bf16),
            pltpu.VMEM((units // 2, features), bf16),
            pltpu.VMEM((slots, own_units), bf16),
            pltpu.VMEM((own_units, slots), bf16),
            pltpu.VMEM((units // 2, features), bf16),
            dma((3,)),
            dma((ring_e,)),
            dma((ring_y,)),
            dma((ring_e,)),
            dma((ring_e,)),
            dma((half_y, 6)),
            dma((half_y, 6)),
            dma((half_y, ring_x - 1)),
            dma((half_y, ring_x - 1)),
            dma((CHUNKS, ring_x)),
            dma((CHUNKS, ring_x)),
            dma((2, CHUNKS, half_y)),
            dma((2, CHUNKS, half_y)),
            dma,
            dma,
            dma((2,)),
        ],
        compiler_params=pltpu.CompilerParams(
            collective_id=0, has_side_effects=True, vmem_limit_bytes=60 * 1024 * 1024
        ),
        cost_estimate=pl.CostEstimate(
            flops=4 * units * slots * features,
            bytes_accessed=2 * units * (slots + 2 * features),
            transcendentals=0,
        ),
    )(
        grad_out,
        gates.T,
        routes.T,
        hidden.reshape(ring_e, cap, units),
        w_down.reshape(ring_y, ring_x, own_units, features),
    )
    hidden_grad, weight_grad = pl.pallas_call(
        hand_over,
        out_shape=(
            jax.ShapeDtypeStruct(hidden_grad.shape, bf16),
            jax.ShapeDtypeStruct(weight_grad.shape, bf16),
        ),
        in_specs=[hbm] * 2,
        out_specs=(hbm, hbm),
        scratch_shapes=[
            pltpu.VMEM(hidden_grad.shape, bf16),
            pltpu.VMEM(weight_grad.shape, bf16),
            dma((2, 2)),
        ],
        compiler_params=pltpu.CompilerParams(vmem_limit_bytes=60 * 1024 * 1024),
    )(hidden_grad, weight_grad)
    return hidden_grad[None, None], weight_grad[None]


def solution(mesh):
    placed = (
        P(("dp", "expert"), "tensor"),
        P(("dp", "expert"), None),
        P(("dp", "expert"), None),
        P("dp", "expert", None, None),
        P("expert", None, "tensor"),
    )
    return jax.shard_map(
        per_device,
        mesh=mesh,
        in_specs=placed,
        out_specs=(P("dp", "expert", "tensor", None), P("expert", "dp", "tensor")),
        check_vma=False,
    )
```

```python
import functools

import jax
import jax.numpy as jnp
from jax import lax
from jax.experimental import pallas as pl
from jax.experimental.pallas import tpu as pltpu
from jax.sharding import PartitionSpec as P

MESH = pl.DeviceIdType.MESH
RING_X = 4
CHUNKS = 4
PIECES = 8
BOUNDS = [0, 3, 5, 8]
SCHEDULE = tuple(
    step
    for steps in (
        ("g0", "g1", "g2", "g3", "s0", "s1"),
        ("s2", "a", "a", "p00", "S0", "p10", "S1", "p20", "S2"),
        ("p30", "S3", "a", "L0", "a", "L1", "a", "L2", "a"),
        ("L3", "p01", "B02", "a", "p11", "B12", "a", "p21", "B22"),
        ("p31", "B32", "p02", "B03", "p12", "B13", "p22", "B23", "p32"),
        ("B33",),
    )
    for step in steps
)


def kernel(
    ring_e,
    ring_x,
    ring_y,
    grad_hbm,
    gates_hbm,
    routes_hbm,
    hidden_ref,
    w_ref,
    hg_hbm,
    wg_hbm,
    grad_ref,
    gates_ref,
    routes_ref,
    saved,
    staged,
    weight,
    arrived,
    outgoing,
    place,
    gate_of,
    flipped,
    prod,
    part_out,
    part_in,
    local,
    other,
    gathered_grad,
    hg_ref,
    wg_ref,
    small_sem,
    saved_sem,
    staged_sem,
    z_send,
    z_recv,
    w_send,
    w_recv,
    f_send,
    f_recv,
    x_send,
    x_recv,
    y_send,
    y_recv,
    g_send,
    g_recv,
    out_sem,
):
    tokens = grad_ref.shape[0]
    cap = arrived.shape[2]
    features = arrived.shape[3]
    group = ring_e // CHUNKS
    rows = group * cap
    half_y = ring_y // 2
    units = prod.shape[3]
    half_units = other.shape[0]

    core = lax.axis_index("dp")
    me = lax.axis_index("expert")
    flat = lax.axis_index("tensor")
    y, x = flat // ring_x, lax.rem(flat, ring_x)
    sibling = {"dp": 1 - core}

    def at_x(step):
        return {"tensor": y * ring_x + lax.rem(x + step + ring_x, ring_x)}

    def at_y(step):
        return {"tensor": lax.rem(y + step + ring_y, ring_y) * ring_x + x}

    offsets = [0, 1, -1, ring_e // 2]
    for offset in range(ring_e // 2 - 1, 1, -1):
        offsets += [offset, -offset]

    def peer(number):
        return lax.rem(me + offsets[number] + ring_e, ring_e)

    def mirror(number):
        if 2 * offsets[number] == ring_e:
            return number
        return offsets.index(-offsets[number])

    def send(src, dst, send_sem, recv_sem, where):
        return pltpu.make_async_remote_copy(
            src_ref=src,
            dst_ref=dst,
            send_sem=send_sem,
            recv_sem=recv_sem,
            device_id=where,
            device_id_type=MESH,
        )

    barrier = pltpu.get_barrier_semaphore()
    for number in range(1, ring_e):
        pl.semaphore_signal(
            barrier, inc=1, device_id={"expert": peer(number)}, device_id_type=MESH
        )
    for step in (1, -1, 2):
        pl.semaphore_signal(barrier, inc=1, device_id=at_x(step), device_id_type=MESH)
    for step in (1, -1):
        pl.semaphore_signal(barrier, inc=1, device_id=at_y(step), device_id_type=MESH)
    pl.semaphore_signal(barrier, inc=1, device_id=sibling, device_id_type=MESH)

    small = [
        pltpu.make_async_copy(src, dst, small_sem.at[index])
        for index, (src, dst) in enumerate(
            ((routes_hbm, routes_ref), (gates_hbm, gates_ref), (grad_hbm, grad_ref))
        )
    ]
    for copy in small:
        copy.start()

    distances = [4, 3, -3, 2, -2, 1, -1, 0]
    bounds = BOUNDS
    parts = [pl.ds(a, b - a) for a, b in zip(bounds, bounds[1:])]
    staged_copies = []
    for index, distance in enumerate(distances):
        copy = pltpu.make_async_copy(
            w_ref.at[lax.rem(y + distance + ring_y, ring_y)],
            staged.at[index],
            staged_sem.at[index],
        )
        copy.start()
        staged_copies.append(copy)
    small[0].wait()
    small[1].wait()

    sublanes = place.shape[0]
    expert_ids = lax.broadcasted_iota(jnp.int32, (sublanes, tokens), 0)
    first = routes_ref[0:1, :] == expert_ids
    second = routes_ref[1:2, :] == expert_ids
    member = jnp.where(first | second, 1.0, 0.0).astype(jnp.bfloat16)
    earlier = jnp.where(
        lax.broadcasted_iota(jnp.int32, (tokens, tokens), 0)
        < lax.broadcasted_iota(jnp.int32, (tokens, tokens), 1),
        1.0,
        0.0,
    ).astype(jnp.bfloat16)
    before = jnp.dot(member, earlier, preferred_element_type=jnp.float32)
    place[...] = jnp.where(first | second, before.astype(jnp.int32), -1)
    gate_of[...] = jnp.where(first, gates_ref[0:1, :], 0.0) + jnp.where(
        second, gates_ref[1:2, :], 0.0
    )

    small[2].wait()

    slot_ids = lax.broadcasted_iota(jnp.int32, (cap, tokens), 0)
    for chunk in range(CHUNKS):
        masks, scales = [], []
        numbers = range(chunk * group, (chunk + 1) * group)
        for number in numbers:
            expert = peer(number)
            hit = slot_ids == place[pl.ds(expert, 1), :]
            masks.append(jnp.where(hit, 1.0, 0.0).astype(jnp.bfloat16))
            scales.append(
                jnp.sum(
                    jnp.where(hit, gate_of[pl.ds(expert, 1), :], 0.0), axis=1, keepdims=True
                )
            )
        picked = jnp.dot(
            jnp.concatenate(masks, axis=0), grad_ref[...], preferred_element_type=jnp.float32
        )
        scaled = (jnp.concatenate(scales, axis=0) * picked).astype(jnp.bfloat16)
        for index, number in enumerate(numbers):
            block = scaled[index * cap : (index + 1) * cap]
            if number == 0:
                arrived[0, 0] = block
            else:
                outgoing[number] = block

    pl.semaphore_wait(barrier, ring_e - 1 + 3 + 2 + 1)

    z_copies = {}
    for number in range(1, ring_e):
        copy = send(
            outgoing.at[number],
            arrived.at[0, mirror(number)],
            z_send.at[number],
            z_recv.at[mirror(number)],
            {"expert": peer(number)},
        )
        z_copies[number] = copy

    half_rows = pl.ds(pl.multiple_of(core * (units // 2), units // 2), units // 2)
    w_copies = {}

    def chip(step):
        return lax.rem(x + step + ring_x, ring_x)

    def send_weight(number):
        part = parts[number]
        for lane, step, slot in ((4, 2, 1), (0, 1, 0), (1, -1, 2)):
            copy = send(
                staged.at[part, chip(step), half_rows],
                weight.at[slot, part, half_rows],
                w_send.at[number, lane],
                w_recv.at[number, lane],
                at_x(step),
            )
            w_copies[number, lane] = copy

    for number in range(len(parts)):
        send_weight(number)

    def start_dispatch():
        for copy in z_copies.values():
            copy.start()

    def start_weight():
        for copy in staged_copies:
            copy.wait()
        for copy in w_copies.values():
            copy.start()

    @pl.when(core == 0)
    def _():
        start_dispatch()
        start_weight()

    @pl.when(core == 1)
    def _():
        start_weight()
        start_dispatch()

    saved_copies = []
    for number in range(ring_e):
        copy = pltpu.make_async_copy(
            hidden_ref.at[peer(number)],
            saved.at[pl.ds(number * cap, cap)],
            saved_sem.at[number],
        )
        copy.start()
        saved_copies.append(copy)

    x_copies, f_copies, y_copies = {}, {}, {}

    def gather(chunk):
        blocks = pl.ds(chunk * group, group)
        for number in range(chunk * group, (chunk + 1) * group):
            if number > 0:
                z_copies[mirror(number)].wait_recv()
        for step, slot in ((2, 2), (1, 1), (-1, 3)):
            copy = send(
                arrived.at[0, blocks],
                arrived.at[slot, blocks],
                x_send.at[chunk, slot],
                x_recv.at[chunk, slot],
                at_x(step),
            )
            copy.start()
            x_copies[chunk, slot] = copy

    def share_weight(number):
        part = parts[number]
        for slot, needed in ((0, (0,)), (2, (1,)), (1, (4,))):
            for lane in needed:
                w_copies[number, lane].wait_recv()
            copy = send(
                weight.at[slot, part, half_rows],
                weight.at[slot, part, half_rows],
                f_send.at[number, slot],
                f_recv.at[number, slot],
                sibling,
            )
            copy.start()
            f_copies[number, slot] = copy

    gathered, shared = set(), set()

    def product(chunk, number):
        if chunk not in gathered:
            gathered.add(chunk)
            for slot in range(1, ring_x):
                x_copies[chunk, slot].wait_recv()
        if number not in shared:
            shared.add(number)
            for slot in range(ring_x - 1):
                f_copies[number, slot].wait_recv()
        blocks = pl.ds(chunk * group, group)
        left = jnp.concatenate(
            [arrived[slot, blocks].reshape(rows, features) for slot in range(ring_x)], axis=1
        )
        right = []
        first, end = bounds[number], bounds[number + 1]
        for index in range(first, end):
            right.append(
                jnp.concatenate(
                    [staged[index, x]] + [weight[slot, index] for slot in range(ring_x - 1)],
                    axis=1,
                )
            )
        product = lax.dot_general(
            left,
            jnp.concatenate(right, axis=0),
            (((1,), (1,)), ((), ())),
            preferred_element_type=jnp.float32,
        )
        for index in range(first, end):
            offset = (index - first) * units
            prod[chunk, index] = product[:, offset : offset + units]

    def message(chunk, lane, slot):
        sign = (1, -1)[lane]
        long = chunk // 2 == lane
        distance = 4 - slot
        takes = (slot - 1,) if slot > (0 if long else 1) else ()
        total = prod[chunk, distances.index(4 if distance == 4 else sign * distance)]
        for taken in takes:
            y_copies[lane, chunk, taken].wait_recv()
            total = total + part_in[lane, chunk, taken].astype(jnp.float32)
        part_out[lane, chunk, slot] = total.astype(jnp.bfloat16)
        copy = send(
            part_out.at[lane, chunk, slot],
            part_in.at[lane, chunk, slot],
            y_send.at[lane, chunk, slot],
            y_recv.at[lane, chunk, slot],
            at_y(sign),
        )
        copy.start()
        y_copies[lane, chunk, slot] = copy

    def start_reduce(chunk):
        long = chunk // 2
        message(chunk, long, 0)
        message(chunk, 1 - long, 1)

    def long_step(chunk):
        message(chunk, chunk // 2, 1)

    def both_step(chunk, slot):
        message(chunk, 0, slot)
        message(chunk, 1, slot)

    def finish(chunk):
        last = 3
        y_copies[0, chunk, last].wait_recv()
        y_copies[1, chunk, last].wait_recv()
        total = (
            prod[chunk, ring_y - 1]
            + part_in[0, chunk, last].astype(jnp.float32)
            + part_in[1, chunk, last].astype(jnp.float32)
        ).astype(jnp.bfloat16)
        for index in range(group):
            source = peer(chunk * group + index)
            gathered_grad[pl.ds(pl.multiple_of(source * cap, cap), cap), :] = total[
                index * cap : (index + 1) * cap
            ]

    piece_units = local.shape[0] // PIECES

    def weight_piece(piece):
        if piece == 0:
            for copy in saved_copies:
                copy.wait()
            flipped[...] = arrived[0].reshape(ring_e * cap, features).T
        base = (1 - core) * half_units if piece < PIECES // 2 else core * half_units
        start = base + (piece % (PIECES // 2)) * piece_units
        start = pl.multiple_of(start, piece_units)
        block = jnp.dot(
            flipped[...],
            saved[:, pl.ds(start, piece_units)],
            preferred_element_type=jnp.float32,
        )
        local[pl.ds(start, piece_units), :] = block.T.astype(jnp.bfloat16)

    theirs = pl.ds(pl.multiple_of((1 - core) * half_units, half_units), half_units)
    ours = pl.ds(pl.multiple_of(core * half_units, half_units), half_units)
    swap = send(local.at[theirs], other, g_send, g_recv, sibling)

    def advance(pieces):
        piece = next(pieces, None)
        if piece is not None:
            weight_piece(piece)
            if piece == PIECES // 2 - 1:
                swap.start()

    pieces = iter(range(PIECES))
    ops = {
        "g": gather,
        "s": share_weight,
        "p": product,
        "S": start_reduce,
        "L": long_step,
        "B": both_step,
        "f": finish,
        "a": lambda: advance(pieces),
    }
    for op in SCHEDULE:
        ops[op[0]](*[int(digit) for digit in op[1:]])

    swap.wait_recv()
    wg_ref[...] = (local[ours].astype(jnp.float32) + other[...].astype(jnp.float32)).astype(
        jnp.bfloat16
    )
    out = pltpu.make_async_copy(wg_ref, wg_hbm, out_sem.at[1])
    out.start()
    for chunk in range(CHUNKS):
        finish(chunk)
    hg_ref[...] = gathered_grad[...].T
    last_out = pltpu.make_async_copy(hg_ref, hg_hbm, out_sem.at[0])
    last_out.start()
    out.wait()
    last_out.wait()

    for copies in (w_copies, z_copies, x_copies, f_copies, y_copies):
        for copy in copies.values():
            copy.wait_send()
    swap.wait_send()


def hand_over(first_in, second_in, first_out, second_out, first, second, sem):
    pairs = ((first_in, first, first_out), (second_in, second, second_out))
    reads = [
        pltpu.make_async_copy(src, here, sem.at[0, index])
        for index, (src, here, _) in enumerate(pairs)
    ]
    writes = [
        pltpu.make_async_copy(here, dst, sem.at[1, index])
        for index, (_, here, dst) in enumerate(pairs)
    ]
    for read in reads:
        read.start()
    for read, write in zip(reads, writes):
        read.wait()
        write.start()
    for write in writes:
        write.wait()


def per_device(grad_out, gates, routes, hidden, w_down):
    ring_e = lax.axis_size("expert")
    ring_t = lax.axis_size("tensor")
    ring_x = RING_X
    ring_y = ring_t // ring_x
    tokens, features = grad_out.shape
    slots, units = hidden.shape[2], hidden.shape[3]
    cap = slots // ring_e
    own_units = units // ring_t
    rows = slots // CHUNKS
    half_y = ring_y // 2
    sublanes = -(-ring_e // 16) * 16
    bf16, f32 = jnp.bfloat16, jnp.float32
    dma = pltpu.SemaphoreType.DMA
    hbm = pl.BlockSpec(memory_space=pl.ANY)
    hidden_grad, weight_grad = pl.pallas_call(
        functools.partial(kernel, ring_e, ring_x, ring_y),
        out_shape=(
            jax.ShapeDtypeStruct((own_units, slots), bf16),
            jax.ShapeDtypeStruct((units // 2, features), bf16),
        ),
        in_specs=[hbm] * 5,
        out_specs=(hbm, hbm),
        scratch_shapes=[
            pltpu.VMEM((tokens, features), bf16),
            pltpu.VMEM((2, tokens), f32),
            pltpu.VMEM((2, tokens), jnp.int32),
            pltpu.VMEM((slots, units), bf16),
            pltpu.VMEM((ring_y, ring_x, own_units, features), bf16),
            pltpu.VMEM((ring_x - 1, ring_y, own_units, features), bf16),
            pltpu.VMEM((ring_x, ring_e, cap, features), bf16),
            pltpu.VMEM((ring_e, cap, features), bf16),
            pltpu.VMEM((sublanes, tokens), jnp.int32),
            pltpu.VMEM((sublanes, tokens), f32),
            pltpu.VMEM((features, slots), bf16),
            pltpu.VMEM((CHUNKS, ring_y, rows, own_units), f32),
            pltpu.VMEM((2, CHUNKS, half_y, rows, own_units), bf16),
            pltpu.VMEM((2, CHUNKS, half_y, rows, own_units), bf16),
            pltpu.VMEM((units, features), bf16),
            pltpu.VMEM((units // 2, features), bf16),
            pltpu.VMEM((slots, own_units), bf16),
            pltpu.VMEM((own_units, slots), bf16),
            pltpu.VMEM((units // 2, features), bf16),
            dma((3,)),
            dma((ring_e,)),
            dma((ring_y,)),
            dma((ring_e,)),
            dma((ring_e,)),
            dma((half_y, 6)),
            dma((half_y, 6)),
            dma((half_y, ring_x - 1)),
            dma((half_y, ring_x - 1)),
            dma((CHUNKS, ring_x)),
            dma((CHUNKS, ring_x)),
            dma((2, CHUNKS, half_y)),
            dma((2, CHUNKS, half_y)),
            dma,
            dma,
            dma((2,)),
        ],
        compiler_params=pltpu.CompilerParams(
            collective_id=0, has_side_effects=True, vmem_limit_bytes=60 * 1024 * 1024
        ),
        cost_estimate=pl.CostEstimate(
            flops=4 * units * slots * features,
            bytes_accessed=2 * units * (slots + 2 * features),
            transcendentals=0,
        ),
    )(
        grad_out,
        gates.T,
        routes.T,
        hidden.reshape(ring_e, cap, units),
        w_down.reshape(ring_y, ring_x, own_units, features),
    )
    hidden_grad, weight_grad = pl.pallas_call(
        hand_over,
        out_shape=(
            jax.ShapeDtypeStruct(hidden_grad.shape, bf16),
            jax.ShapeDtypeStruct(weight_grad.shape, bf16),
        ),
        in_specs=[hbm] * 2,
        out_specs=(hbm, hbm),
        scratch_shapes=[
            pltpu.VMEM(hidden_grad.shape, bf16),
            pltpu.VMEM(weight_grad.shape, bf16),
            dma((2, 2)),
        ],
        compiler_params=pltpu.CompilerParams(vmem_limit_bytes=60 * 1024 * 1024),
    )(hidden_grad, weight_grad)
    return hidden_grad[None, None], weight_grad[None]


def solution(mesh):
    placed = (
        P(("dp", "expert"), "tensor"),
        P(("dp", "expert"), None),
        P(("dp", "expert"), None),
        P("dp", "expert", None, None),
        P("expert", None, "tensor"),
    )
    return jax.shard_map(
        per_device,
        mesh=mesh,
        in_specs=placed,
        out_specs=(P("dp", "expert", "tensor", None), P("expert", "dp", "tensor")),
        check_vma=False,
    )
```
